128 devices in a mesh: section: 8 (over x, core), expert: 16 (over z, y).
Axes of the slice: x: 4, y: 4, z: 4, core: 2. Of those that a mesh axis runs over, the one named last changes fastest.
Arguments:
- sent_acts: bfloat16 [8, 1024, 2048], P('section', 'expert'), may hold values from -6 to 6
- stash: bfloat16 [8, 1024, 2048], P('section', 'expert'), may hold values from -6 to 6
- cotangents: bfloat16 [8, 1024, 2048], P('section', 'expert'), may hold values from -6 to 6
- norm_gain: bfloat16 [8, 2048], P('section'), may hold values from 0.5 to 1.5
- w_gate: bfloat16 [8, 16, 2048, 768], P('section', 'expert'), may hold values from -0.125 to 0.125
- w_up: bfloat16 [8, 16, 2048, 768], P('section', 'expert'), may hold values from -0.125 to 0.125
- w_down: bfloat16 [8, 16, 768, 2048], P('section', 'expert'), may hold values from -0.21875 to 0.21875
- routes_next: int32 [8, 1024, 8], P('section', 'expert'), may hold values from 0 to 15, all different within a row; in each aligned block of 64 rows (0 to 63, 64 to 127, ..., all dimensions but the last counted through in order) at most 48 rows name the same one
- gates_next: bfloat16 [8, 1024, 8], P('section', 'expert'), may hold values from 0.049804688 to 0.5
- routes_prev: int32 [8, 1024, 8], P('section', 'expert'), may hold values from 0 to 15, all different within a row; in each aligned block of 64 rows (0 to 63, 64 to 127, ..., all dimensions but the last counted through in order) at most 48 rows name the same one
- gates_prev: bfloat16 [8, 1024, 8], P('section', 'expert'), may hold values from 0.049804688 to 0.5
Outputs:
- fwd_out: bfloat16 [8, 1024, 2048], P('section', 'expert')
- bwd_out: bfloat16 [8, 1024, 2048], P('section', 'expert')
- gate_grad: bfloat16 [8, 1024, 8], P('section', 'expert')
- grad_w_gate: bfloat16 [8, 16, 2048, 768], P('section', 'expert')
- grad_w_up: bfloat16 [8, 16, 2048, 768], P('section', 'expert')
- grad_w_down: bfloat16 [8, 16, 768, 2048], P('section', 'expert')
The draws below stay inside these ranges and needn't reach their ends.
Inputs may be any that keep to these rules, and one draw needn't show every extreme that they name: `routes_next`: each row names 8 different experts. At most 48 of the 64 tokens of one device choose one expert, and in some device's tokens some expert is chosen by exactly 48. `routes_prev`: each row names 8 different experts. At most 48 of the 64 tokens of one device choose one expert, and in some device's tokens some expert is chosen by exactly 48.
All inputs are finite; a program needn't handle non-finite values.
Results may differ from the reference program's by a relative error of at most 0.008.
Values may be sent and summed in bfloat16 or wider, within the bound.
No kernel may reach another device: no remote copies, remote signals or barrier semaphores. Data moves between devices by JAX's collectives and lax.ppermute only.
A program may use at most 128 MiB of HBM per device.

```python
import math
import jax
import jax.numpy as jnp
import numpy as np
from jax import lax

D = 2048
FF = 768
EXPERTS = 16
TOP = 8
TOK_DEV = 64
SECTIONS = 8
TOKENS = 1024
CAP = 48
N_EXPERT = 16


def level_of(own_key, dims, split, low, top_value):
    def one(dim, blocks):
        heights = jax.random.uniform(jax.random.fold_in(jax.random.fold_in(own_key, 6), dim), (blocks,), jnp.float32, low / len(split), top_value / len(split))
        return jnp.repeat(jnp.exp(heights), dims[dim] // blocks).reshape((-1,) + (1,) * (len(dims) - dim - 1))

    gain = one(*split[0])
    for cut in split[1:]:
        gain = gain * one(*cut)
    return gain


def routed_block(stream_key, own, number, rows, number_of, top, limit, lean):
    ranking = jax.random.permutation(stream_key, number_of)
    packed, common = portions_of(number_of, rows * top, limit, lean, True), portions_of(number_of, rows * top, limit, lean, False)
    places = jnp.arange(number_of)

    def named(sizes, offset_by):
        used = int((sizes > 0).sum())
        fixed = max(1, used // 4)
        shifted = fixed + (places - fixed + offset_by * (used - fixed)) % max(1, number_of - fixed)
        return jnp.zeros((number_of,), jnp.int32).at[ranking[jnp.where(places < fixed, places, shifted)]].set(jnp.asarray(sizes, jnp.int32))

    sizes = jnp.where(number % 4 == 0, named(packed, number // 4), named(common, number - number // 4 - 1))
    mixed = jax.random.permutation(jax.random.fold_in(own, 3), number_of)
    donor, taker = mixed[0:number_of // 2 * 2:2], mixed[1:number_of // 2 * 2:2]
    slack = jnp.minimum(sizes[donor] - 1, limit - sizes[taker]) // 2
    slack = jnp.where((donor == ranking[0]) | (taker == ranking[0]) | (sizes[taker] == 0), 0, jnp.maximum(slack, 0))
    shifted = jax.random.randint(jax.random.fold_in(own, 4), (number_of // 2,), 0, 1 << 20) % (slack + 1)
    sizes = sizes.at[donor].add(-shifted).at[taker].add(shifted)
    items = jnp.searchsorted(jnp.cumsum(sizes), jnp.arange(rows * top), side="right").astype(jnp.int32)
    table = items.reshape(top, rows).T
    table = table[jax.random.permutation(jax.random.fold_in(own, 1), rows)]
    offset_by = jax.random.randint(jax.random.fold_in(own, 2), (rows, 1), 0, top)
    return jnp.take_along_axis(table, (jnp.arange(top)[None, :] + offset_by) % top, axis=1)


def portions_of(number_of, total, reach, skew, full):
    loads = [(1 << 20) // math.isqrt(standing ** skew) + 1 for standing in range(1, number_of + 1)]
    largest = reach if full else min(reach, max(-(-total // number_of), total * loads[0] // sum(loads)))
    least = 1 if total - largest >= number_of - 1 else 0
    given, surplus = [largest] + [least] * (number_of - 1), total - largest - least * (number_of - 1)
    while surplus > 0:
        movable = [i for i in range(1, number_of) if given[i] < largest] or [i for i in range(1, number_of) if given[i] < reach]
        mass, left = sum([loads[i] for i in movable]), surplus
        for i in movable:
            more = min(reach - given[i], max(1, left * loads[i] // mass), surplus)
            given[i] = given[i] + more
            surplus = surplus - more
    return np.array(given)


def noise(own_key, shape, spread, bound, cuts=(), held_as=jnp.bfloat16):
    entries = jax.random.normal(own_key, shape, jnp.float32) * spread
    if len(cuts) > 0:
        entries = level_of(own_key, shape, cuts, -0.22, 0.18) * entries
    return jnp.clip(entries, min=-bound, max=bound).astype(held_as)


def setup_inputs(seed: int = 0) -> dict:
    key_list = jax.random.split(jax.random.key(seed), 12)
    sent_acts = noise(key_list[0], (SECTIONS, TOKENS, D), 1.0, 6.0, ((0, 8), (1, 16)))
    stash = noise(key_list[1], (SECTIONS, TOKENS, D), 1.0, 6.0, ((0, 8), (1, 16)))
    cotangents = noise(key_list[2], (SECTIONS, TOKENS, D), 1.0, 6.0, ((0, 8), (1, 16)))
    norm_gain = jnp.clip(1.0 + 0.1 * jax.random.normal(key_list[3], (SECTIONS, D), jnp.float32), 0.5, 1.5).astype(jnp.bfloat16)
    w_gate = noise(key_list[4], (SECTIONS, EXPERTS, D, FF), D ** -0.5, 0.125, ((0, 8), (1, 16)))
    w_up = noise(key_list[5], (SECTIONS, EXPERTS, D, FF), D ** -0.5, 0.125, ((0, 8), (1, 16)))
    w_down = noise(key_list[6], (SECTIONS, EXPERTS, FF, D), FF ** -0.5, 0.21875, ((0, 8), (1, 16)))
    routes_next_keys = jax.random.split(jax.random.fold_in(key_list[7], 1), SECTIONS * TOKENS // TOK_DEV)
    routes_next_turns = jax.random.permutation(jax.random.fold_in(key_list[7], 3), SECTIONS * TOKENS // TOK_DEV)
    routes_next = jax.vmap(lambda own, number: routed_block(jax.random.fold_in(key_list[7], 2), own, number, TOK_DEV, EXPERTS, TOP, CAP, 2))(routes_next_keys, routes_next_turns).reshape((SECTIONS, TOKENS, TOP))
    gates_next = jnp.clip(jnp.exp(math.log(0.5) - 2.306499 * jax.random.uniform(key_list[8], (SECTIONS, TOKENS, TOP), jnp.float32) ** level_of(key_list[8], (SECTIONS, TOKENS, TOP), ((0, 8), (1, 16)), -0.2, 0.2)), 0.049804688, 0.5).astype(jnp.bfloat16)
    routes_prev_keys = jax.random.split(jax.random.fold_in(key_list[9], 1), SECTIONS * TOKENS // TOK_DEV)
    routes_prev_turns = jax.random.permutation(jax.random.fold_in(key_list[9], 3), SECTIONS * TOKENS // TOK_DEV)
    routes_prev = jax.vmap(lambda own, number: routed_block(jax.random.fold_in(key_list[9], 2), own, number, TOK_DEV, EXPERTS, TOP, CAP, 2))(routes_prev_keys, routes_prev_turns).reshape((SECTIONS, TOKENS, TOP))
    gates_prev = jnp.clip(jnp.exp(math.log(0.5) - 2.306499 * jax.random.uniform(key_list[10], (SECTIONS, TOKENS, TOP), jnp.float32) ** level_of(key_list[10], (SECTIONS, TOKENS, TOP), ((0, 8), (1, 16)), -0.2, 0.2)), 0.049804688, 0.5).astype(jnp.bfloat16)
    return {"sent_acts": sent_acts, "stash": stash, "cotangents": cotangents, "norm_gain": norm_gain, "w_gate": w_gate, "w_up": w_up, "w_down": w_down, "routes_next": routes_next, "gates_next": gates_next, "routes_prev": routes_prev, "gates_prev": gates_prev}


EPS = 1e-06

def apply_rms_norm(rows, norm_scale_weight):
    value_entries = rows.astype(jnp.float32)
    inverse_root_scale = lax.rsqrt(lax.optimization_barrier(jnp.mean(value_entries * value_entries, axis=-1, keepdims=True)) + EPS)
    unit_rows = value_entries * inverse_root_scale
    normalized_rows = (unit_rows * norm_scale_weight.astype(jnp.float32)).astype(jnp.bfloat16)
    return (normalized_rows, unit_rows, inverse_root_scale)

def place_slots(routes):
    flat = routes.reshape(-1).astype(jnp.int32)
    onehot = (flat[:, None] == jnp.arange(EXPERTS, dtype=jnp.int32)[None, :]).astype(jnp.int32)
    before = jnp.cumsum(onehot, axis=0) - onehot
    slot = lax.optimization_barrier(jnp.sum(before * onehot, axis=1)).astype(jnp.int32)
    return (flat, slot)

def dispatch(rows, flat, slot):

    def one_block(block_rows, block_flat, block_slot):
        buffer = jnp.zeros((EXPERTS, CAP) + block_rows.shape[1:], block_rows.dtype)
        return buffer.at[block_flat, block_slot].set(block_rows)
    buffers = jax.vmap(one_block)(rows, flat, slot)
    return jnp.swapaxes(buffers, 0, 1)

def collect(buffers, flat, slot):
    per_block = jnp.swapaxes(buffers, 0, 1)
    return jax.vmap(lambda block, block_flat, block_slot: block[block_flat, block_slot])(per_block, flat, slot)

def expert_forward(args):
    rows, weight_gate, weight_up, weight_down = args
    pre_gate = jnp.dot(rows, weight_gate, preferred_element_type=jnp.float32)
    pre_up = jnp.dot(rows, weight_up, preferred_element_type=jnp.float32)
    hidden = (jax.nn.silu(pre_gate) * pre_up).astype(jnp.bfloat16)
    return jnp.dot(hidden, weight_down, preferred_element_type=jnp.float32).astype(jnp.bfloat16)

def expert_backward(args):
    rows, out_grad, weight_gate, weight_up, weight_down = args
    pre_gate = jnp.dot(rows, weight_gate, preferred_element_type=jnp.float32)
    pre_up = jnp.dot(rows, weight_up, preferred_element_type=jnp.float32)
    sigma = jax.nn.sigmoid(pre_gate)
    active = pre_gate * sigma
    hidden = (active * pre_up).astype(jnp.bfloat16)
    expert_out = jnp.dot(hidden, weight_down, preferred_element_type=jnp.float32).astype(jnp.bfloat16)
    d_hidden = jnp.dot(out_grad, weight_down.T, preferred_element_type=jnp.float32)
    d_gate = (d_hidden * pre_up * sigma * (1.0 + pre_gate * (1.0 - sigma))).astype(jnp.bfloat16)
    d_up = (d_hidden * active).astype(jnp.bfloat16)
    row_grad = (jnp.dot(d_gate, weight_gate.T, preferred_element_type=jnp.float32) + jnp.dot(d_up, weight_up.T, preferred_element_type=jnp.float32)).astype(jnp.bfloat16)
    grad_gate = jnp.dot(rows.T, d_gate, preferred_element_type=jnp.float32).astype(jnp.bfloat16)
    grad_up = jnp.dot(rows.T, d_up, preferred_element_type=jnp.float32).astype(jnp.bfloat16)
    grad_down = jnp.dot(hidden.T, out_grad, preferred_element_type=jnp.float32).astype(jnp.bfloat16)
    return (expert_out, row_grad, grad_gate, grad_up, grad_down)

def reference(sent_acts, stash, cotangents, norm_gain, w_gate, w_up, w_down, routes_next, gates_next, routes_prev, gates_prev):
    fwd_list, bwd_list, gate_list, wg_list, wu_list, wd_list = ([], [], [], [], [], [])
    for section_index in range(SECTIONS):
        norm_scale_weight = norm_gain[section_index]
        weight_gate, weight_up, weight_down = (w_gate[section_index], w_up[section_index], w_down[section_index])
        arrived = sent_acts[(section_index - 1) % SECTIONS]
        normalized_rows, _, _ = apply_rms_norm(arrived, norm_scale_weight)
        flat, slot = jax.vmap(place_slots)(routes_next[section_index].reshape(N_EXPERT, TOK_DEV, TOP))
        rows = jnp.repeat(normalized_rows, TOP, axis=0).reshape(N_EXPERT, TOK_DEV * TOP, D)
        buffers = dispatch(rows, flat, slot).reshape(EXPERTS, N_EXPERT * CAP, D)
        outputs = lax.map(expert_forward, (buffers, weight_gate, weight_up, weight_down))
        picked = collect(outputs.reshape(EXPERTS, N_EXPERT, CAP, D), flat, slot).reshape(TOKENS, TOP, D)
        mixed = lax.optimization_barrier(jnp.sum(gates_next[section_index].astype(jnp.float32)[..., None] * picked.astype(jnp.float32), axis=1))
        fwd_list.append((arrived.astype(jnp.float32) + mixed).astype(jnp.bfloat16))
        received_rows = cotangents[(section_index + 1) % SECTIONS]
        previous_normalized_rows, unit_rows, inverse_root_scale = apply_rms_norm(stash[section_index], norm_scale_weight)
        flat_prev, slot_prev = jax.vmap(place_slots)(routes_prev[section_index].reshape(N_EXPERT, TOK_DEV, TOP))
        rows_prev = jnp.repeat(previous_normalized_rows, TOP, axis=0).reshape(N_EXPERT, TOK_DEV * TOP, D)
        out_grad = (gates_prev[section_index].astype(jnp.float32)[..., None] * received_rows.astype(jnp.float32)[:, None, :]).astype(jnp.bfloat16)
        out_grad = out_grad.reshape(N_EXPERT, TOK_DEV * TOP, D)
        row_buffers = dispatch(rows_prev, flat_prev, slot_prev).reshape(EXPERTS, N_EXPERT * CAP, D)
        grad_buffers = dispatch(out_grad, flat_prev, slot_prev).reshape(EXPERTS, N_EXPERT * CAP, D)
        expert_out, row_grad, grad_gate, grad_up, grad_down = lax.map(expert_backward, (row_buffers, grad_buffers, weight_gate, weight_up, weight_down))
        out_pick = collect(expert_out.reshape(EXPERTS, N_EXPERT, CAP, D), flat_prev, slot_prev).reshape(TOKENS, TOP, D)
        selected_gradient = collect(row_grad.reshape(EXPERTS, N_EXPERT, CAP, D), flat_prev, slot_prev).reshape(TOKENS, TOP, D)
        gate_list.append(lax.optimization_barrier(jnp.sum(out_pick.astype(jnp.float32) * received_rows.astype(jnp.float32)[:, None, :], axis=-1)).astype(jnp.bfloat16))
        normalized_gradient = lax.optimization_barrier(jnp.sum(selected_gradient.astype(jnp.float32), axis=1)) * norm_scale_weight.astype(jnp.float32)
        backward_result = received_rows.astype(jnp.float32) + inverse_root_scale * (normalized_gradient - unit_rows * lax.optimization_barrier(jnp.mean(normalized_gradient * unit_rows, axis=-1, keepdims=True)))
        bwd_list.append(backward_result.astype(jnp.bfloat16))
        wg_list.append(grad_gate)
        wu_list.append(grad_up)
        wd_list.append(grad_down)
    return (jnp.stack(fwd_list), jnp.stack(bwd_list), jnp.stack(gate_list), jnp.stack(wg_list), jnp.stack(wu_list), jnp.stack(wd_list))
```

```python
import jax
import jax.numpy as jnp
from jax import lax
from jax.sharding import PartitionSpec as P

CAP = 48
EPS = 1e-06
LANES = 128
BF16 = jnp.bfloat16
F32 = jnp.float32


def shifted(array, axis, by):
    count = lax.axis_size(axis)
    return lax.ppermute(array, axis, [(i, (i + by) % count) for i in range(count)])


def mm(a, b, dims):
    return lax.dot_general(a, b, (dims, ((), ())), preferred_element_type=F32)


def rms_norm(rows, gain):
    values = rows.astype(F32)
    scale = lax.rsqrt(jnp.mean(values * values, axis=-1, keepdims=True) + EPS)
    unit = values * scale
    return (unit * gain).astype(BF16), unit, scale


def tables(routes, gates, experts):
    tokens = routes.shape[0]
    hit = (routes[:, :, None] == jnp.arange(experts, dtype=jnp.int32)[None, None, :]).astype(F32)
    chosen = jnp.sum(hit, axis=1)
    gate = jnp.sum(hit * gates.astype(F32)[:, :, None], axis=1)
    row = lax.broadcasted_iota(jnp.int32, (tokens, tokens), 0)
    col = lax.broadcasted_iota(jnp.int32, (tokens, tokens), 1)
    upto = (col <= row).astype(BF16)
    rank = mm(upto, chosen.astype(BF16), ((1,), (0,))) * chosen
    return hit, rank, gate


def spread_columns(experts):
    owner = lax.broadcasted_iota(jnp.int32, (experts, experts, CAP), 1)
    mine = lax.broadcasted_iota(jnp.int32, (experts, experts, CAP), 0)
    return (owner == mine).astype(BF16).reshape(experts, experts * CAP)


def pick_matrix(rank, columns, experts):
    place = lax.broadcasted_iota(jnp.int32, (1, experts, CAP), 2).astype(F32).reshape(1, experts * CAP) + 1.0
    return mm(rank.astype(BF16), columns, ((1,), (0,))) == place


def per_device(
    sent_acts,
    stash,
    cotangents,
    norm_gain,
    w_gate,
    w_up,
    w_down,
    routes_next,
    gates_next,
    routes_prev,
    gates_prev,
):
    experts = lax.axis_size("expert") * w_gate.shape[1]
    me = lax.axis_index("expert")
    gain = norm_gain[0].astype(F32)
    wg, wu, wd = w_gate[0, 0], w_up[0, 0], w_down[0, 0]
    tokens, width = sent_acts.shape[1:]
    blocks = experts
    columns = spread_columns(experts)

    cot = shifted(cotangents, "section", -1)[0]
    arrived = shifted(sent_acts, "section", 1)[0]

    prev_rows, unit_prev, scale_prev = rms_norm(stash[0], gain)
    hit_prev, rank_prev, gate_prev = tables(routes_prev[0], gates_prev[0], experts)
    extra = jnp.pad(gate_prev.astype(BF16), ((0, 0), (0, LANES - experts)))
    bundle = jnp.concatenate([prev_rows, cot, extra], axis=1)
    gathered = lax.all_gather(bundle, "expert", axis=0, tiled=True)

    next_rows, _, _ = rms_norm(arrived, gain)
    _, rank_next, gate_next = tables(routes_next[0], gates_next[0], experts)
    pick_next = pick_matrix(rank_next, columns, experts)
    send = mm(pick_next.astype(BF16), next_rows, ((0,), (0,))).astype(BF16)
    recv = lax.all_to_all(
        send.reshape(experts, CAP, width), "expert", split_axis=0, concat_axis=0, tiled=True
    ).reshape(blocks * CAP, width)
    pre_gate = mm(recv, wg, ((1,), (0,)))
    pre_up = mm(recv, wu, ((1,), (0,)))
    hidden = (jax.nn.silu(pre_gate) * pre_up).astype(BF16)
    out = mm(hidden, wd, ((1,), (0,))).astype(BF16)
    back = lax.all_to_all(
        out.reshape(blocks, CAP, width), "expert", split_axis=0, concat_axis=0, tiled=True
    ).reshape(experts * CAP, width)
    blend = jnp.where(pick_next, mm(gate_next.astype(BF16), columns, ((1,), (0,))), 0.0).astype(BF16)
    fwd_out = (arrived.astype(F32) + mm(blend, back, ((1,), (0,)))).astype(BF16)

    rows = gathered[:, :width]
    cots = gathered[:, width : 2 * width]
    gates = gathered[:, 2 * width :].astype(F32)
    lane = lax.broadcasted_iota(jnp.int32, gates.shape, 1)
    gate = jnp.sum(jnp.where(lane == me, gates, 0.0), axis=1, keepdims=True)
    pre_gate = mm(rows, wg, ((1,), (0,)))
    pre_up = mm(rows, wu, ((1,), (0,)))
    plain = mm(cots, wd, ((1,), (1,)))
    sigma = jax.nn.sigmoid(pre_gate)
    active = pre_gate * sigma
    hidden = (active * pre_up).astype(BF16)
    d_hidden = plain * gate
    d_gate = (d_hidden * pre_up * sigma * (1.0 + pre_gate * (1.0 - sigma))).astype(BF16)
    d_up = (d_hidden * active).astype(BF16)
    gated = (hidden.astype(F32) * gate).astype(BF16)
    token_dots = jnp.sum(hidden.astype(F32) * plain, axis=1).astype(BF16)

    taken = (gate > 0.0).astype(F32).reshape(blocks, tokens)
    row = lax.broadcasted_iota(jnp.int32, (tokens, tokens), 0)
    col = lax.broadcasted_iota(jnp.int32, (tokens, tokens), 1)
    rank = mm(taken.astype(BF16), (row <= col).astype(BF16), ((1,), (0,))) * taken
    place = lax.broadcasted_iota(jnp.int32, (1, CAP, 1), 1).astype(F32) + 1.0
    pack = (rank[:, None, :] == place).astype(BF16)

    both = jnp.concatenate([d_gate, d_up], axis=1).reshape(blocks, tokens, -1)
    both = jnp.einsum("bct,btf->bcf", pack, both, preferred_element_type=F32).astype(BF16)
    both = both.reshape(blocks * CAP, -1)
    ff = wg.shape[1]
    row_grad = (
        mm(both[:, :ff], wg, ((1,), (1,))) + mm(both[:, ff:], wu, ((1,), (1,)))
    ).astype(BF16)
    grads = lax.all_to_all(
        row_grad.reshape(blocks, CAP, width), "expert", split_axis=0, concat_axis=0, tiled=True
    ).reshape(experts * CAP, width)
    dots = lax.all_gather(token_dots, "expert", axis=0, tiled=True).reshape(experts, blocks, tokens)

    grad_gate = mm(rows, d_gate, ((0,), (0,))).astype(BF16)
    grad_up = mm(rows, d_up, ((0,), (0,))).astype(BF16)
    grad_down = mm(gated, cots, ((0,), (0,))).astype(BF16)

    mine = lax.dynamic_index_in_dim(dots, me, axis=1, keepdims=False).astype(F32)
    gate_grad = jnp.sum(hit_prev * mine.T[:, None, :], axis=2).astype(BF16)

    pick_prev = pick_matrix(rank_prev, columns, experts).astype(BF16)
    summed = mm(pick_prev, grads, ((1,), (0,)))
    dxhat = summed * gain
    bwd_out = cot.astype(F32) + scale_prev * (
        dxhat - unit_prev * jnp.mean(dxhat * unit_prev, axis=-1, keepdims=True)
    )
    return (
        fwd_out[None],
        bwd_out.astype(BF16)[None],
        gate_grad[None],
        grad_gate[None, None],
        grad_up[None, None],
        grad_down[None, None],
    )


def solution(mesh):
    tokens = P("section", "expert", None)
    weight = P("section", "expert", None, None)
    return jax.shard_map(
        per_device,
        mesh=mesh,
        in_specs=(tokens, tokens, tokens, P("section", None), weight, weight, weight, tokens, tokens, tokens, tokens),
        out_specs=(tokens, tokens, tokens, weight, weight, weight),
        check_vma=False,
    )
```

```python
import functools
import math

import jax
import jax.numpy as jnp
from jax import lax
from jax.experimental import pallas as pl
from jax.experimental.pallas import tpu as pltpu
from jax.sharding import PartitionSpec as P

CAP = 48
EPS = 1e-06
LANES = 128
BF16 = jnp.bfloat16
F32 = jnp.float32
NN = ((1,), (0,))
NT = ((1,), (1,))
TN = ((0,), (0,))
SIDE = 4
GRANT = 48 * 1024 * 1024


def shifted(array, axis, by):
    count = lax.axis_size(axis)
    return lax.ppermute(array, axis, [(i, (i + by) % count) for i in range(count)])


def pull(array, along, d):
    if d % SIDE == 0:
        return array
    pairs = []
    for i in range(SIDE * SIDE):
        z, y = divmod(i, SIDE)
        source = ((z + d) % SIDE) * SIDE + y if along == "z" else z * SIDE + (y + d) % SIDE
        pairs.append((source, i))
    return lax.ppermute(array, "expert", pairs)


def mm(a, b, dims=NN):
    return lax.dot_general(a, b, (dims, ((), ())), preferred_element_type=F32)


def rms_norm(rows, gain):
    values = rows.astype(F32)
    scale = lax.rsqrt(jnp.mean(values * values, axis=-1, keepdims=True) + EPS)
    unit = values * scale
    return (unit * gain).astype(BF16), unit, scale


def dense_gates(routes, gates, experts):
    lane = jnp.arange(experts, dtype=jnp.int32)
    hit = (routes[:, :, None] == lane[None, None, :]).astype(F32)
    return hit, jnp.sum(hit * gates.astype(F32)[:, :, None], axis=1).astype(BF16)


def iota(shape, dim):
    return lax.broadcasted_iota(jnp.int32, shape, dim)


def ranks(table, tokens):
    rows = table.shape[0]
    taken = (table.astype(F32) > 0.0).astype(F32)
    row, col = iota((rows, rows), 0), iota((rows, rows), 1)
    upto = jnp.where((col <= row) & (col // tokens == row // tokens), 1.0, 0.0).astype(BF16)
    return mm(upto, taken.astype(BF16)) * taken


def pick_lane(array, lane):
    return jnp.sum(jnp.where(iota(array.shape, 1) == lane, array.astype(F32), 0.0), axis=1, keepdims=True)


def packing(table, lane, tokens):
    rows = table.shape[0]
    blocks = rows // tokens
    rank = pick_lane(ranks(table, tokens), lane)
    slot = iota((rows, blocks * CAP), 1)
    same = iota((rows, blocks * CAP), 0) // tokens == slot // CAP
    hit = same & (rank == ((slot % CAP) + 1).astype(F32))
    return jnp.where(hit, 1.0, 0.0).T.astype(BF16)


def backward_kernel(tokens, width, pos, gathered, wg, wu, wd, *rest):
    pieces, (d_gate_out, d_up_out, gated_out) = rest[:SIDE], rest[SIDE : SIDE + 3]
    held, wg_v, wu_v, wd_v, sems, weight_sems = rest[SIDE + 3 :]
    me, y = pos[0], pos[2]
    group = SIDE * tokens
    wide = held.shape[1]

    def source(d, zb):
        return (zb * SIDE + lax.rem(y + d, SIDE)) * tokens

    def block_copy(d, zb):
        return pltpu.make_async_copy(
            gathered.at[pl.ds(pl.multiple_of(source(d, zb), tokens), tokens), pl.ds(0, wide)],
            held.at[pl.ds(pl.multiple_of(d * group + zb * tokens, tokens), tokens), :],
            sems.at[d * SIDE + zb],
        )

    weights = [
        pltpu.make_async_copy(hbm, vmem, weight_sems.at[k])
        for k, (hbm, vmem) in enumerate(((wg, wg_v), (wu, wu_v), (wd, wd_v)))
    ]
    weights[0].start()
    for zb in range(SIDE):
        block_copy(0, zb).start()
    weights[1].start()
    weights[2].start()
    for d in range(1, SIDE):
        for zb in range(SIDE):
            block_copy(d, zb).start()
    for copy in weights:
        copy.wait()

    def tile(d, carry):
        for zb in range(SIDE):
            block_copy(d, zb).wait()
        at = pl.ds(pl.multiple_of(d * group, group), group)
        table = held[at, 2 * width :]
        gate = pick_lane(table, me)
        pack = packing(table, me, tokens)
        pre_gate = mm(held[at, :width], wg_v[...])
        pre_up = mm(held[at, :width], wu_v[...])
        plain = mm(held[at, width : 2 * width], wd_v[...], NT)
        sigma = jax.nn.sigmoid(pre_gate)
        active = pre_gate * sigma
        hidden = (active * pre_up).astype(BF16).astype(F32)
        d_hidden = plain * gate
        d_gate = (d_hidden * pre_up * sigma * (1.0 + pre_gate * (1.0 - sigma))).astype(BF16)
        d_up = (d_hidden * active).astype(BF16)
        gated = (hidden * gate).astype(BF16)
        dots = jnp.sum(hidden * plain, axis=1, keepdims=True)
        dots = jnp.where(iota((group, LANES), 1) == me, dots, 0.0).astype(BF16)
        for zb in range(SIDE):
            cut = slice(zb * tokens, (zb + 1) * tokens)
            to = pl.ds(pl.multiple_of(source(d, zb), tokens), tokens)
            d_gate_out[to, :] = d_gate[cut]
            d_up_out[to, :] = d_up[cut]
            gated_out[to, :] = gated[cut]
        gate_rows = mm(pack, d_gate).astype(BF16)
        up_rows = mm(pack, d_up).astype(BF16)
        dot_rows = mm(pack, dots).astype(BF16)
        grad = (mm(gate_rows, wg_v[...], NT) + mm(up_rows, wu_v[...], NT)).astype(BF16)
        for k in range(SIDE):

            @pl.when(d == k)
            def _():
                pieces[k][:, :width] = grad
                pieces[k][:, width:] = dot_rows

        return carry

    lax.fori_loop(0, SIDE, tile, 0)


def forward_kernel(tokens, width, offset, lane, pos, gathered, wg, wu, wd, *rest):
    pieces = rest[:SIDE]
    held, packed, wg_v, wu_v, wd_v, sems, weight_sems = rest[SIDE:]
    me, z = pos[0], pos[1]
    group = SIDE * tokens
    rows = SIDE * CAP
    wide = held.shape[1]

    def block_copy(d):
        start = pl.multiple_of(lax.rem(z + d, SIDE) * group, group)
        return pltpu.make_async_copy(
            gathered.at[pl.ds(start, group), pl.ds(offset, wide)],
            held.at[pl.ds(pl.multiple_of(d * group, group), group), :],
            sems.at[d],
        )

    weights = [
        pltpu.make_async_copy(hbm, vmem, weight_sems.at[k])
        for k, (hbm, vmem) in enumerate(((wg, wg_v), (wu, wu_v), (wd, wd_v)))
    ]
    for d in range(SIDE):
        block_copy(d).start()
    for copy in weights:
        copy.start()

    def pack_tile(d, carry):
        block_copy(d).wait()
        at = pl.ds(pl.multiple_of(d * group, group), group)
        pack = packing(held[at, :LANES], me + lane, tokens)
        to = pl.ds(pl.multiple_of(d * rows, rows), rows)
        packed[to, :] = mm(pack, held[at, LANES:]).astype(BF16)
        return carry

    lax.fori_loop(0, SIDE, pack_tile, 0)
    for copy in weights:
        copy.wait()

    def tile(c, carry):
        at = pl.ds(pl.multiple_of(c * 2 * rows, 2 * rows), 2 * rows)
        pre_gate = mm(packed[at, :], wg_v[...])
        pre_up = mm(packed[at, :], wu_v[...])
        hidden = (pre_gate * jax.nn.sigmoid(pre_gate) * pre_up).astype(BF16)
        out = mm(hidden, wd_v[...]).astype(BF16)
        for k in range(SIDE // 2):

            @pl.when(c == k)
            def _():
                pieces[2 * k][...] = out[:rows]
                pieces[2 * k + 1][...] = out[rows:]

        return carry

    lax.fori_loop(0, SIDE // 2, tile, 0)


def combine_kernel(tokens, along, offset, lane, weighted, pos, gathered, *rest):
    rows, outs, (tables, sems) = rest[:SIDE], rest[SIDE : 2 * SIDE], rest[2 * SIDE :]
    z, y = pos[1], pos[2]

    def block_of(d):
        return lax.rem((z if along == "y" else y) + d, SIDE)

    def copy(d):
        b = block_of(d)
        start = (b * SIDE + y) if along == "y" else (z * SIDE + b)
        return pltpu.make_async_copy(
            gathered.at[pl.ds(pl.multiple_of(start * tokens, tokens), tokens), pl.ds(offset, LANES)],
            tables.at[d],
            sems.at[d],
        )

    for d in range(SIDE):
        copy(d).start()
    column = iota((LANES, SIDE * CAP), 1)
    owner = jnp.zeros((LANES, SIDE * CAP), jnp.int32)
    for j in range(SIDE):
        if along == "y":
            expert = z * SIDE + lax.rem(y + SIDE - j, SIDE)
        else:
            expert = lax.rem(z + SIDE - j, SIDE) * SIDE + y
        owner = jnp.where(column // CAP == j, expert + lane, owner)
    spread = jnp.where(iota((LANES, SIDE * CAP), 0) == owner, 1.0, 0.0).astype(BF16)
    place = ((iota((tokens, SIDE * CAP), 1) % CAP) + 1).astype(F32)
    for d in range(SIDE):
        copy(d).wait()
        table = tables[d]
        here = mm(ranks(table, tokens).astype(BF16), spread) == place
        value = mm(table, spread) if weighted else 1.0
        matrix = jnp.where(here, value, 0.0).astype(BF16)
        at = pl.ds(pl.multiple_of(block_of(d) * CAP, CAP), CAP)
        mine = jnp.concatenate([part[at, :] for part in rows], axis=0)
        outs[d][...] = mm(matrix, mine).astype(BF16)


ANY = pl.BlockSpec(memory_space=pl.ANY)
VMEM = pl.BlockSpec(memory_space=pltpu.VMEM)
SMEM = pl.BlockSpec(memory_space=pltpu.SMEM)


def per_device(
    sent_acts,
    stash,
    cotangents,
    norm_gain,
    w_gate,
    w_up,
    w_down,
    routes_next,
    gates_next,
    routes_prev,
    gates_prev,
):
    experts = lax.axis_size("expert")
    me = lax.axis_index("expert")
    pos = jnp.stack([me, me // SIDE, me % SIDE]).astype(jnp.int32)
    gain = norm_gain[0].astype(F32)
    wg, wu, wd = w_gate[0, 0], w_up[0, 0], w_down[0, 0]
    tokens, width = sent_acts.shape[1:]
    ff = wg.shape[1]
    everyone = experts * tokens
    rows = SIDE * CAP
    params = pltpu.CompilerParams(vmem_limit_bytes=GRANT)

    cot = shifted(cotangents[0], "section", -1)
    arrived = shifted(sent_acts[0], "section", 1)
    prev_rows, unit_prev, scale_prev = rms_norm(stash[0], gain)
    hit_prev, table_prev = dense_gates(routes_prev[0], gates_prev[0], experts)
    _, table_next = dense_gates(routes_next[0], gates_next[0], experts)
    table = jnp.pad(jnp.concatenate([table_prev, table_next], axis=1), ((0, 0), (0, LANES - 2 * experts)))
    next_rows, _, _ = rms_norm(arrived, gain)
    bundle = jnp.concatenate([prev_rows, cot, table, next_rows], axis=1)
    gathered = lax.all_gather(bundle, "expert", axis=0, tiled=True)
    table_at = 2 * width

    weight_scratch = [
        pltpu.VMEM(wg.shape, BF16),
        pltpu.VMEM(wu.shape, BF16),
        pltpu.VMEM(wd.shape, BF16),
    ]
    unit = 2 * width * ff
    *pieces, d_gate, d_up, gated = pl.pallas_call(
        functools.partial(backward_kernel, tokens, width),
        out_shape=[jax.ShapeDtypeStruct((rows, width + LANES), BF16)] * SIDE
        + [jax.ShapeDtypeStruct((everyone, ff), BF16)] * 3,
        in_specs=[SMEM] + [ANY] * 4,
        out_specs=[VMEM] * (SIDE + 3),
        scratch_shapes=[pltpu.VMEM((everyone, 2 * width + LANES), BF16)]
        + weight_scratch
        + [pltpu.SemaphoreType.DMA((SIDE * SIDE,)), pltpu.SemaphoreType.DMA((3,))],
        compiler_params=params,
        cost_estimate=pl.CostEstimate(
            flops=(3 * everyone + 2 * SIDE * rows) * unit,
            bytes_accessed=26 * 1024 * 1024,
            transcendentals=everyone * ff,
        ),
        name="expert_backward",
    )(pos, gathered, wg, wu, wd)
    grads = [pull(pieces[d], "y", SIDE - d) for d in range(SIDE)]

    pieces = pl.pallas_call(
        functools.partial(forward_kernel, tokens, width, table_at, experts),
        out_shape=[jax.ShapeDtypeStruct((rows, width), BF16)] * SIDE,
        in_specs=[SMEM] + [ANY] * 4,
        out_specs=[VMEM] * SIDE,
        scratch_shapes=[
            pltpu.VMEM((everyone, width + LANES), BF16),
            pltpu.VMEM((SIDE * rows, width), BF16),
        ]
        + weight_scratch
        + [pltpu.SemaphoreType.DMA((SIDE,)), pltpu.SemaphoreType.DMA((3,))],
        compiler_params=params,
        cost_estimate=pl.CostEstimate(
            flops=3 * SIDE * rows * unit, bytes_accessed=18 * 1024 * 1024, transcendentals=SIDE * rows * ff
        ),
        name="expert_forward",
    )(pos, gathered, wg, wu, wd)
    outs = [pull(pieces[d], "z", SIDE - d) for d in range(SIDE)]

    def combine(parts, along, lane, weighted):
        wide = parts[0].shape[1]
        return pl.pallas_call(
            functools.partial(combine_kernel, tokens, along, table_at, lane, weighted),
            out_shape=[jax.ShapeDtypeStruct((tokens, wide), BF16)] * SIDE,
            in_specs=[SMEM, ANY] + [VMEM] * SIDE,
            out_specs=[VMEM] * SIDE,
            scratch_shapes=[pltpu.VMEM((SIDE, tokens, LANES), BF16), pltpu.SemaphoreType.DMA((SIDE,))],
            compiler_params=params,
            cost_estimate=pl.CostEstimate(
                flops=2 * SIDE * tokens * rows * wide, bytes_accessed=5 * 1024 * 1024, transcendentals=0
            ),
            name="combine_" + along,
        )(pos, gathered, *parts)

    partial = combine(grads, "y", 0, False)
    summed = sum(pull(partial[d], "z", SIDE - d).astype(F32) for d in range(SIDE))
    partial = combine(outs, "z", experts, True)
    mixed = sum(pull(partial[d], "y", SIDE - d).astype(F32) for d in range(SIDE))
    fwd_out = (arrived.astype(F32) + mixed).astype(BF16)

    grad_gate = mm(gathered[:, :width], d_gate, TN).astype(BF16)
    grad_up = mm(gathered[:, :width], d_up, TN).astype(BF16)
    grad_down = mm(gated, gathered[:, width : 2 * width], TN).astype(BF16)

    gate_grad = jnp.sum(hit_prev * summed[:, None, width : width + experts], axis=2).astype(BF16)
    dxhat = summed[:, :width] * gain
    bwd_out = cot.astype(F32) + scale_prev * (
        dxhat - unit_prev * jnp.mean(dxhat * unit_prev, axis=-1, keepdims=True)
    )
    return (
        fwd_out[None],
        bwd_out.astype(BF16)[None],
        gate_grad[None],
        grad_gate[None, None],
        grad_up[None, None],
        grad_down[None, None],
    )


def solution(mesh):
    tokens = P("section", "expert", None)
    weight = P("section", "expert", None, None)
    return jax.shard_map(
        per_device,
        mesh=mesh,
        in_specs=(tokens, tokens, tokens, P("section", None), weight, weight, weight, tokens, tokens, tokens, tokens),
        out_specs=(tokens, tokens, tokens, weight, weight, weight),
        check_vma=False,
    )
```

```python
import functools
import math

import jax
import jax.numpy as jnp
from jax import lax
from jax.experimental import pallas as pl
from jax.experimental.pallas import tpu as pltpu
from jax.sharding import PartitionSpec as P

CAP = 48
EPS = 1e-06
LANES = 128
BF16 = jnp.bfloat16
F32 = jnp.float32
NN = ((1,), (0,))
NT = ((1,), (1,))
TN = ((0,), (0,))
SIDE = 4
GRANT = 48 * 1024 * 1024


def shifted(array, axis, by):
    count = lax.axis_size(axis)
    return lax.ppermute(array, axis, [(i, (i + by) % count) for i in range(count)])


def pull(array, along, d):
    if d % SIDE == 0:
        return array
    pairs = []
    for i in range(SIDE * SIDE):
        z, y = divmod(i, SIDE)
        source = ((z + d) % SIDE) * SIDE + y if along == "z" else z * SIDE + (y + d) % SIDE
        pairs.append((source, i))
    return lax.ppermute(array, "expert", pairs)


def mm(a, b, dims=NN):
    return lax.dot_general(a, b, (dims, ((), ())), preferred_element_type=F32)


def rms_norm(rows, gain):
    values = rows.astype(F32)
    scale = lax.rsqrt(jnp.mean(values * values, axis=-1, keepdims=True) + EPS)
    unit = values * scale
    return (unit * gain).astype(BF16), unit, scale


def dense_gates(routes, gates, experts):
    lane = jnp.arange(experts, dtype=jnp.int32)
    hit = (routes[:, :, None] == lane[None, None, :]).astype(F32)
    return hit, jnp.sum(hit * gates.astype(F32)[:, :, None], axis=1).astype(BF16)


def iota(shape, dim):
    return lax.broadcasted_iota(jnp.int32, shape, dim)


def ranks(table, tokens):
    rows = table.shape[0]
    taken = (table.astype(F32) > 0.0).astype(F32)
    row, col = iota((rows, rows), 0), iota((rows, rows), 1)
    upto = jnp.where((col <= row) & (col // tokens == row // tokens), 1.0, 0.0).astype(BF16)
    return mm(upto, taken.astype(BF16)) * taken


def pick_lane(array, lane):
    return jnp.sum(jnp.where(iota(array.shape, 1) == lane, array.astype(F32), 0.0), axis=1, keepdims=True)


def packing(table, lane, tokens):
    rows = table.shape[0]
    blocks = rows // tokens
    rank = pick_lane(ranks(table, tokens), lane)
    slot = iota((rows, blocks * CAP), 1)
    same = iota((rows, blocks * CAP), 0) // tokens == slot // CAP
    hit = same & (rank == ((slot % CAP) + 1).astype(F32))
    return jnp.where(hit, 1.0, 0.0).T.astype(BF16)


def weight_copies(refs, held, sems):
    return [pltpu.make_async_copy(hbm, vmem, sems.at[k]) for k, (hbm, vmem) in enumerate(zip(refs, held))]


def pack_lines(tokens, table, lane, out, rows):
    group = SIDE * tokens
    count = SIDE * CAP
    gates = []
    for k in range(table.shape[0] // group):
        at = slice(k * group, (k + 1) * group)
        pack = packing(table[at, :], lane, tokens)
        out[k * count : (k + 1) * count, :] = mm(pack, rows[at, :]).astype(BF16)
        gates.append(pick_lane(mm(pack, table[at, :]), lane))
    return jnp.concatenate(gates, axis=0)


def backward_kernel(tokens, width, pos, both, table, wg, wu, wd, *rest):
    pieces, (d_gate_out, d_up_out, gated_out, packed) = rest[:SIDE], rest[SIDE : SIDE + 4]
    grads, wg_v, wu_v, wd_v, sems, piece_sems = rest[SIDE + 4 :]
    me, z = pos[0], pos[1]
    step = pl.program_id(0)
    first = step == 0
    slots = packed.shape[0]
    lines = slots // (SIDE * CAP)

    def piece_copy(k):
        source = lax.rem(z + k, SIDE) * SIDE * CAP
        return pltpu.make_async_copy(
            grads.at[pl.ds(pl.multiple_of(source, SIDE * CAP), SIDE * CAP), :], pieces[k], piece_sems.at[k]
        )

    copies = weight_copies((wg, wu, wd), (wg_v, wu_v, wd_v), sems)

    @pl.when(first)
    def _():
        for copy in copies:
            copy.start()

    gate = pack_lines(tokens, table, me, packed, both)

    @pl.when(first)
    def _():
        copies[0].wait()

    pre_gate = mm(packed[:, :width], wg_v[...])

    @pl.when(first)
    def _():
        copies[1].wait()
        copies[2].wait()

    pre_up = mm(packed[:, :width], wu_v[...])
    plain = mm(packed[:, width:], wd_v[...], NT)
    sigma = jax.nn.sigmoid(pre_gate)
    active = pre_gate * sigma
    hidden = (active * pre_up).astype(BF16).astype(F32)
    d_hidden = plain * gate
    d_gate = (d_hidden * pre_up * sigma * (1.0 + pre_gate * (1.0 - sigma))).astype(BF16)
    d_up = (d_hidden * active).astype(BF16)
    d_gate_out[...] = d_gate
    d_up_out[...] = d_up
    gated_out[...] = (hidden * gate).astype(BF16)
    dots = jnp.sum(hidden * plain, axis=1, keepdims=True)
    here = pl.ds(pl.multiple_of(step * slots, slots), slots)
    grads[here, width:] = jnp.where(iota((slots, LANES), 1) == me, dots, 0.0).astype(BF16)
    grads[here, :width] = (mm(d_gate, wg_v[...], NT) + mm(d_up, wu_v[...], NT)).astype(BF16)
    for k in range(SIDE):

        @pl.when(lax.rem(z + k, SIDE) // lines == step)
        def _():
            piece_copy(k).start()

    @pl.when(step == pl.num_programs(0) - 1)
    def _():
        for k in range(SIDE):
            piece_copy(k).wait()


def forward_kernel(tokens, width, offset, lane, pos, gathered, wg, wu, wd, *rest):
    pieces = rest[:SIDE]
    held, packed, wg_v, wu_v, wd_v, sems, weight_sems = rest[SIDE:]
    me, y = pos[0], pos[2]
    group = SIDE * tokens
    rows = SIDE * CAP
    wide = held.shape[1]

    def block_copy(d, zb):
        start = pl.multiple_of((zb * SIDE + lax.rem(y + d, SIDE)) * tokens, tokens)
        return pltpu.make_async_copy(
            gathered.at[pl.ds(start, tokens), pl.ds(offset, wide)],
            held.at[pl.ds(pl.multiple_of(d * group + zb * tokens, tokens), tokens), :],
            sems.at[d * SIDE + zb],
        )

    weights = [
        pltpu.make_async_copy(hbm, vmem, weight_sems.at[k])
        for k, (hbm, vmem) in enumerate(((wg, wg_v), (wu, wu_v), (wd, wd_v)))
    ]
    for d in range(SIDE):
        for zb in range(SIDE):
            block_copy(d, zb).start()
    for copy in weights:
        copy.start()

    def pack_tile(d, carry):
        for zb in range(SIDE):
            block_copy(d, zb).wait()
        at = pl.ds(pl.multiple_of(d * group, group), group)
        pack = packing(held[at, :LANES], me + lane, tokens)
        to = pl.ds(pl.multiple_of(d * rows, rows), rows)
        packed[to, :] = mm(pack, held[at, LANES:]).astype(BF16)
        return carry

    lax.fori_loop(0, SIDE, pack_tile, 0)
    for copy in weights:
        copy.wait()

    def tile(c, carry):
        at = pl.ds(pl.multiple_of(c * 2 * rows, 2 * rows), 2 * rows)
        pre_gate = mm(packed[at, :], wg_v[...])
        pre_up = mm(packed[at, :], wu_v[...])
        hidden = (pre_gate * jax.nn.sigmoid(pre_gate) * pre_up).astype(BF16)
        out = mm(hidden, wd_v[...]).astype(BF16)
        for k in range(SIDE // 2):

            @pl.when(c == k)
            def _():
                pieces[2 * k][...] = out[:rows]
                pieces[2 * k + 1][...] = out[rows:]

        return carry

    lax.fori_loop(0, SIDE // 2, tile, 0)


def combine_kernel(tokens, along, offset, lane, weighted, pos, gathered, *rest):
    rows, outs, (tables, sems) = rest[:SIDE], rest[SIDE : 2 * SIDE], rest[2 * SIDE :]
    z, y = pos[1], pos[2]

    def block_of(d):
        return lax.rem((z if along == "y" else y) + d, SIDE)

    def copy(d):
        b = block_of(d)
        start = (b * SIDE + y) if along == "y" else (z * SIDE + b)
        return pltpu.make_async_copy(
            gathered.at[pl.ds(pl.multiple_of(start * tokens, tokens), tokens), pl.ds(offset, LANES)],
            tables.at[d],
            sems.at[d],
        )

    for d in range(SIDE):
        copy(d).start()
    column = iota((LANES, SIDE * CAP), 1)
    owner = jnp.zeros((LANES, SIDE * CAP), jnp.int32)
    for j in range(SIDE):
        if along == "y":
            expert = z * SIDE + lax.rem(y + SIDE - j, SIDE)
        else:
            expert = lax.rem(z + SIDE - j, SIDE) * SIDE + y
        owner = jnp.where(column // CAP == j, expert + lane, owner)
    spread = jnp.where(iota((LANES, SIDE * CAP), 0) == owner, 1.0, 0.0).astype(BF16)
    place = ((iota((tokens, SIDE * CAP), 1) % CAP) + 1).astype(F32)
    for d in range(SIDE):
        copy(d).wait()
        table = tables[d]
        here = mm(ranks(table, tokens).astype(BF16), spread) == place
        value = mm(table, spread) if weighted else 1.0
        matrix = jnp.where(here, value, 0.0).astype(BF16)
        at = pl.ds(pl.multiple_of(block_of(d) * CAP, CAP), CAP)
        mine = jnp.concatenate([part[at, :] for part in rows], axis=0)
        outs[d][...] = mm(matrix, mine).astype(BF16)


ANY = pl.BlockSpec(memory_space=pl.ANY)
VMEM = pl.BlockSpec(memory_space=pltpu.VMEM)
SMEM = pl.BlockSpec(memory_space=pltpu.SMEM)


def per_device(
    sent_acts,
    stash,
    cotangents,
    norm_gain,
    w_gate,
    w_up,
    w_down,
    routes_next,
    gates_next,
    routes_prev,
    gates_prev,
):
    experts = lax.axis_size("expert")
    me = lax.axis_index("expert")
    pos = jnp.stack([me, me // SIDE, me % SIDE]).astype(jnp.int32)
    gain = norm_gain[0].astype(F32)
    wg, wu, wd = w_gate[0, 0], w_up[0, 0], w_down[0, 0]
    tokens, width = sent_acts.shape[1:]
    ff = wg.shape[1]
    everyone = experts * tokens
    rows = SIDE * CAP
    params = pltpu.CompilerParams(vmem_limit_bytes=GRANT)

    cot = shifted(cotangents[0], "section", -1)
    arrived = shifted(sent_acts[0], "section", 1)
    prev_rows, unit_prev, scale_prev = rms_norm(stash[0], gain)
    hit_prev, table_prev = dense_gates(routes_prev[0], gates_prev[0], experts)
    _, table_next = dense_gates(routes_next[0], gates_next[0], experts)
    table = jnp.pad(jnp.concatenate([table_prev, table_next], axis=1), ((0, 0), (0, LANES - 2 * experts)))
    next_rows, _, _ = rms_norm(arrived, gain)
    bundle = jnp.concatenate([prev_rows, cot, table, next_rows], axis=1)
    gathered = lax.all_gather(bundle, "expert", axis=0, tiled=True)
    table_at = 2 * width

    weight_scratch = [
        pltpu.VMEM(wg.shape, BF16),
        pltpu.VMEM(wu.shape, BF16),
        pltpu.VMEM(wd.shape, BF16),
    ]
    unit = 2 * width * ff
    pieces = pl.pallas_call(
        functools.partial(forward_kernel, tokens, width, table_at, experts),
        out_shape=[jax.ShapeDtypeStruct((rows, width), BF16)] * SIDE,
        in_specs=[SMEM] + [ANY] * 4,
        out_specs=[VMEM] * SIDE,
        scratch_shapes=[
            pltpu.VMEM((everyone, width + LANES), BF16),
            pltpu.VMEM((SIDE * rows, width), BF16),
        ]
        + weight_scratch
        + [pltpu.SemaphoreType.DMA((SIDE * SIDE,)), pltpu.SemaphoreType.DMA((3,))],
        compiler_params=params,
        cost_estimate=pl.CostEstimate(
            flops=3 * SIDE * rows * unit, bytes_accessed=18 * 1024 * 1024, transcendentals=SIDE * rows * ff
        ),
        name="expert_forward",
    )(pos, gathered, wg, wu, wd)
    outs = [pull(pieces[d], "y", SIDE - d) for d in range(SIDE)]

    after, _ = lax.optimization_barrier((pos, pieces))
    steps = 2
    group, slots = everyone // steps, experts * CAP // steps
    wide = width + LANES

    def slot_spec(columns):
        return pl.BlockSpec((slots, columns), lambda i: (i, 0))

    *pieces, d_gate, d_up, gated, packed = pl.pallas_call(
        functools.partial(backward_kernel, tokens, width),
        grid=(steps,),
        out_shape=[jax.ShapeDtypeStruct((rows, wide), BF16)] * SIDE
        + [jax.ShapeDtypeStruct((experts * CAP, ff), BF16)] * 3
        + [jax.ShapeDtypeStruct((experts * CAP, 2 * width), BF16)],
        in_specs=[
            SMEM,
            pl.BlockSpec((group, 2 * width), lambda i: (i, 0)),
            pl.BlockSpec((group, LANES), lambda i: (i, table_at // LANES)),
        ]
        + [ANY] * 3,
        out_specs=[ANY] * SIDE + [slot_spec(ff)] * 3 + [slot_spec(2 * width)],
        scratch_shapes=[pltpu.VMEM((experts * CAP, wide), BF16)]
        + weight_scratch
        + [
            pltpu.SemaphoreType.DMA((3,)),
            pltpu.SemaphoreType.DMA((SIDE,)),
        ],
        compiler_params=params,
        cost_estimate=pl.CostEstimate(
            flops=5 * SIDE * rows * unit, bytes_accessed=26 * 1024 * 1024, transcendentals=SIDE * rows * ff
        ),
        name="expert_backward",
    )(after, gathered, gathered, wg, wu, wd)
    grads = [pull(pieces[d], "z", SIDE - d) for d in range(SIDE)]

    tables = gathered[:, table_at : table_at + LANES]

    def combine(at, parts, along, lane, weighted):
        wide = parts[0].shape[1]
        return pl.pallas_call(
            functools.partial(combine_kernel, tokens, along, 0, lane, weighted),
            out_shape=[jax.ShapeDtypeStruct((tokens, wide), BF16)] * SIDE,
            in_specs=[SMEM, ANY] + [VMEM] * SIDE,
            out_specs=[VMEM] * SIDE,
            scratch_shapes=[pltpu.VMEM((SIDE, tokens, LANES), BF16), pltpu.SemaphoreType.DMA((SIDE,))],
            compiler_params=params,
            cost_estimate=pl.CostEstimate(
                flops=2 * SIDE * tokens * rows * wide, bytes_accessed=5 * 1024 * 1024, transcendentals=0
            ),
            name="combine_" + along,
        )(at, tables, *parts)

    grad_gate = mm(packed[:, :width], d_gate, TN).astype(BF16)
    grad_up = mm(packed[:, :width], d_up, TN).astype(BF16)

    partial = combine(pos, outs, "y", experts, True)
    mixed = sum(pull(partial[d], "z", SIDE - d).astype(F32) for d in range(SIDE))
    fwd_out = (arrived.astype(F32) + mixed).astype(BF16)

    later, grad_gate, grad_up = lax.optimization_barrier((pos, grad_gate, grad_up))
    partial = combine(later, grads, "z", 0, False)
    gated, partial = lax.optimization_barrier((gated, partial))
    summed = sum(pull(partial[d], "y", SIDE - d).astype(F32) for d in range(SIDE))
    grad_down = mm(gated, packed[:, width:], TN).astype(BF16)

    gate_grad = jnp.sum(hit_prev * summed[:, None, width : width + experts], axis=2).astype(BF16)
    dxhat = summed[:, :width] * gain
    bwd_out = cot.astype(F32) + scale_prev * (
        dxhat - unit_prev * jnp.mean(dxhat * unit_prev, axis=-1, keepdims=True)
    )
    return (
        fwd_out[None],
        bwd_out.astype(BF16)[None],
        gate_grad[None],
        grad_gate[None, None],
        grad_up[None, None],
        grad_down[None, None],
    )


def solution(mesh):
    tokens = P("section", "expert", None)
    weight = P("section", "expert", None, None)
    return jax.shard_map(
        per_device,
        mesh=mesh,
        in_specs=(tokens, tokens, tokens, P("section", None), weight, weight, weight, tokens, tokens, tokens, tokens),
        out_specs=(tokens, tokens, tokens, weight, weight, weight),
        check_vma=False,
    )
```

```python
import functools
import math

import jax
import jax.numpy as jnp
from jax import lax
from jax.experimental import pallas as pl
from jax.experimental.pallas import tpu as pltpu
from jax.sharding import PartitionSpec as P

CAP = 48
EPS = 1e-06
LANES = 128
BF16 = jnp.bfloat16
F32 = jnp.float32
NN = ((1,), (0,))
NT = ((1,), (1,))
TN = ((0,), (0,))
SIDE = 4
GRANT = 48 * 1024 * 1024


def shifted(array, axis, by):
    count = lax.axis_size(axis)
    return lax.ppermute(array, axis, [(i, (i + by) % count) for i in range(count)])


def pull(array, along, d):
    if d % SIDE == 0:
        return array
    pairs = []
    for i in range(SIDE * SIDE):
        z, y = divmod(i, SIDE)
        source = ((z + d) % SIDE) * SIDE + y if along == "z" else z * SIDE + (y + d) % SIDE
        pairs.append((source, i))
    return lax.ppermute(array, "expert", pairs)


def mm(a, b, dims=NN):
    return lax.dot_general(a, b, (dims, ((), ())), preferred_element_type=F32)


def rms_norm(rows, gain):
    values = rows.astype(F32)
    scale = lax.rsqrt(jnp.mean(values * values, axis=-1, keepdims=True) + EPS)
    unit = values * scale
    return (unit * gain).astype(BF16), unit, scale


def dense_gates(routes, gates, experts):
    lane = jnp.arange(experts, dtype=jnp.int32)
    hit = (routes[:, :, None] == lane[None, None, :]).astype(F32)
    return hit, jnp.sum(hit * gates.astype(F32)[:, :, None], axis=1).astype(BF16)


def iota(shape, dim):
    return lax.broadcasted_iota(jnp.int32, shape, dim)


def ranks(table, tokens):
    rows = table.shape[0]
    taken = (table.astype(F32) > 0.0).astype(F32)
    row, col = iota((rows, rows), 0), iota((rows, rows), 1)
    upto = jnp.where((col <= row) & (col // tokens == row // tokens), 1.0, 0.0).astype(BF16)
    return mm(upto, taken.astype(BF16)) * taken


def pick_lane(array, lane):
    return jnp.sum(jnp.where(iota(array.shape, 1) == lane, array.astype(F32), 0.0), axis=1, keepdims=True)


def packing(table, lane, tokens):
    rows = table.shape[0]
    blocks = rows // tokens
    rank = pick_lane(ranks(table, tokens), lane)
    slot = iota((rows, blocks * CAP), 1)
    same = iota((rows, blocks * CAP), 0) // tokens == slot // CAP
    hit = same & (rank == ((slot % CAP) + 1).astype(F32))
    return jnp.where(hit, 1.0, 0.0).T.astype(BF16)


def weight_copies(refs, held, sems):
    return [pltpu.make_async_copy(hbm, vmem, sems.at[k]) for k, (hbm, vmem) in enumerate(zip(refs, held))]


def pack_lines(tokens, table, lane, out, rows):
    group = SIDE * tokens
    count = SIDE * CAP
    gates = []
    for k in range(table.shape[0] // group):
        at = slice(k * group, (k + 1) * group)
        pack = packing(table[at, :], lane, tokens)
        out[k * count : (k + 1) * count, :] = mm(pack, rows[at, :]).astype(BF16)
        gates.append(pick_lane(mm(pack, table[at, :]), lane))
    return jnp.concatenate(gates, axis=0)


def backward_kernel(tokens, width, pos, both, table, wg, wu, wd, *rest):
    pieces, (d_gate_out, d_up_out, gated_out, packed) = rest[:SIDE], rest[SIDE : SIDE + 4]
    grads, wg_v, wu_v, wd_v, sems, piece_sems = rest[SIDE + 4 :]
    me, z = pos[0], pos[1]
    step = pl.program_id(0)
    first = step == 0
    slots = packed.shape[0]
    lines = slots // (SIDE * CAP)

    def piece_copy(k):
        source = lax.rem(z + k, SIDE) * SIDE * CAP
        return pltpu.make_async_copy(
            grads.at[pl.ds(pl.multiple_of(source, SIDE * CAP), SIDE * CAP), :], pieces[k], piece_sems.at[k]
        )

    copies = weight_copies((wg, wu, wd), (wg_v, wu_v, wd_v), sems)

    @pl.when(first)
    def _():
        for copy in copies:
            copy.start()

    gate = pack_lines(tokens, table, me, packed, both)

    @pl.when(first)
    def _():
        copies[0].wait()

    pre_gate = mm(packed[:, :width], wg_v[...])

    @pl.when(first)
    def _():
        copies[1].wait()
        copies[2].wait()

    pre_up = mm(packed[:, :width], wu_v[...])
    plain = mm(packed[:, width:], wd_v[...], NT)
    sigma = jax.nn.sigmoid(pre_gate)
    active = pre_gate * sigma
    hidden = (active * pre_up).astype(BF16).astype(F32)
    d_hidden = plain * gate
    d_gate = (d_hidden * pre_up * sigma * (1.0 + pre_gate * (1.0 - sigma))).astype(BF16)
    d_up = (d_hidden * active).astype(BF16)
    d_gate_out[...] = d_gate
    d_up_out[...] = d_up
    gated_out[...] = (hidden * gate).astype(BF16)
    dots = jnp.sum(hidden * plain, axis=1, keepdims=True)
    here = pl.ds(pl.multiple_of(step * slots, slots), slots)
    grads[here, width:] = jnp.where(iota((slots, LANES), 1) == me, dots, 0.0).astype(BF16)
    grads[here, :width] = (mm(d_gate, wg_v[...], NT) + mm(d_up, wu_v[...], NT)).astype(BF16)
    for k in range(SIDE):

        @pl.when(lax.rem(z + k, SIDE) // lines == step)
        def _():
            piece_copy(k).start()

    @pl.when(step == pl.num_programs(0) - 1)
    def _():
        for k in range(SIDE):
            piece_copy(k).wait()


def forward_kernel(tokens, width, offset, lane, pos, gathered, wg, wu, wd, *rest):
    out, held, packed, wg_v, wu_v, wd_v, sems, weight_sems = rest
    me = pos[0]
    group = SIDE * tokens
    rows = SIDE * CAP
    wide = held.shape[1]

    def block_copy(d, zb):
        start = pl.multiple_of((zb * SIDE + d) * tokens, tokens)
        return pltpu.make_async_copy(
            gathered.at[pl.ds(start, tokens), pl.ds(offset, wide)],
            held.at[pl.ds(pl.multiple_of(d * group + zb * tokens, tokens), tokens), :],
            sems.at[d * SIDE + zb],
        )

    weights = [
        pltpu.make_async_copy(hbm, vmem, weight_sems.at[k])
        for k, (hbm, vmem) in enumerate(((wg, wg_v), (wu, wu_v), (wd, wd_v)))
    ]
    for d in range(SIDE):
        for zb in range(SIDE):
            block_copy(d, zb).start()
    for copy in weights:
        copy.start()

    def pack_tile(d, carry):
        for zb in range(SIDE):
            block_copy(d, zb).wait()
        at = pl.ds(pl.multiple_of(d * group, group), group)
        pack = packing(held[at, :LANES], me + lane, tokens)
        to = pl.ds(pl.multiple_of(d * rows, rows), rows)
        packed[to, :] = mm(pack, held[at, LANES:]).astype(BF16)
        return carry

    lax.fori_loop(0, SIDE, pack_tile, 0)
    for copy in weights:
        copy.wait()

    def tile(c, carry):
        at = pl.ds(pl.multiple_of(c * 2 * rows, 2 * rows), 2 * rows)
        pre_gate = mm(packed[at, :], wg_v[...])
        pre_up = mm(packed[at, :], wu_v[...])
        hidden = (pre_gate * jax.nn.sigmoid(pre_gate) * pre_up).astype(BF16)
        out[at, :] = mm(hidden, wd_v[...]).astype(BF16)
        return carry

    lax.fori_loop(0, SIDE // 2, tile, 0)


def combine_kernel(tokens, along, offset, lane, weighted, whole, pos, gathered, *rest):
    parts = 1 if whole else SIDE
    rows, outs, (tables, sems) = rest[:parts], rest[parts : 2 * parts], rest[2 * parts :]
    if whole:
        rows = [rest[0].at[pl.ds(j * SIDE * CAP, SIDE * CAP), :] for j in range(SIDE)]
    z, y = pos[1], pos[2]

    def block_of(d):
        return lax.rem((z if along == "y" else y) + d, SIDE)

    def copy(d):
        b = block_of(d)
        start = (b * SIDE + y) if along == "y" else (z * SIDE + b)
        return pltpu.make_async_copy(
            gathered.at[pl.ds(pl.multiple_of(start * tokens, tokens), tokens), pl.ds(offset, LANES)],
            tables.at[d],
            sems.at[d],
        )

    for d in range(SIDE):
        copy(d).start()
    column = iota((LANES, SIDE * CAP), 1)
    owner = jnp.zeros((LANES, SIDE * CAP), jnp.int32)
    for j in range(SIDE):
        if along == "y":
            expert = z * SIDE + (j if whole else lax.rem(y + SIDE - j, SIDE))
        else:
            expert = lax.rem(z + SIDE - j, SIDE) * SIDE + y
        owner = jnp.where(column // CAP == j, expert + lane, owner)
    spread = jnp.where(iota((LANES, SIDE * CAP), 0) == owner, 1.0, 0.0).astype(BF16)
    place = ((iota((tokens, SIDE * CAP), 1) % CAP) + 1).astype(F32)
    for d in range(SIDE):
        copy(d).wait()
        table = tables[d]
        here = mm(ranks(table, tokens).astype(BF16), spread) == place
        value = mm(table, spread) if weighted else 1.0
        matrix = jnp.where(here, value, 0.0).astype(BF16)
        at = pl.ds(pl.multiple_of(block_of(d) * CAP, CAP), CAP)
        mine = jnp.concatenate([part[at, :] for part in rows], axis=0)
        if whole:
            outs[0][pl.ds(pl.multiple_of(block_of(d) * tokens, tokens), tokens), :] = mm(matrix, mine).astype(BF16)
        else:
            outs[d][...] = mm(matrix, mine).astype(BF16)


ANY = pl.BlockSpec(memory_space=pl.ANY)
VMEM = pl.BlockSpec(memory_space=pltpu.VMEM)
SMEM = pl.BlockSpec(memory_space=pltpu.SMEM)


def per_device(
    sent_acts,
    stash,
    cotangents,
    norm_gain,
    w_gate,
    w_up,
    w_down,
    routes_next,
    gates_next,
    routes_prev,
    gates_prev,
):
    experts = lax.axis_size("expert")
    me = lax.axis_index("expert")
    pos = jnp.stack([me, me // SIDE, me % SIDE]).astype(jnp.int32)
    gain = norm_gain[0].astype(F32)
    wg, wu, wd = w_gate[0, 0], w_up[0, 0], w_down[0, 0]
    tokens, width = sent_acts.shape[1:]
    ff = wg.shape[1]
    everyone = experts * tokens
    rows = SIDE * CAP
    params = pltpu.CompilerParams(vmem_limit_bytes=GRANT)

    cot = shifted(cotangents[0], "section", -1)
    arrived = shifted(sent_acts[0], "section", 1)
    prev_rows, unit_prev, scale_prev = rms_norm(stash[0], gain)
    hit_prev, table_prev = dense_gates(routes_prev[0], gates_prev[0], experts)
    _, table_next = dense_gates(routes_next[0], gates_next[0], experts)
    table = jnp.pad(jnp.concatenate([table_prev, table_next], axis=1), ((0, 0), (0, LANES - 2 * experts)))
    next_rows, _, _ = rms_norm(arrived, gain)
    bundle = jnp.concatenate([prev_rows, cot, table, next_rows], axis=1)
    gathered = lax.all_gather(bundle, "expert", axis=0, tiled=True)
    table_at = 2 * width

    weight_scratch = [
        pltpu.VMEM(wg.shape, BF16),
        pltpu.VMEM(wu.shape, BF16),
        pltpu.VMEM(wd.shape, BF16),
    ]
    unit = 2 * width * ff
    out = pl.pallas_call(
        functools.partial(forward_kernel, tokens, width, table_at, experts),
        out_shape=jax.ShapeDtypeStruct((SIDE * rows, width), BF16),
        in_specs=[SMEM] + [ANY] * 4,
        out_specs=VMEM,
        scratch_shapes=[
            pltpu.VMEM((everyone, width + LANES), BF16),
            pltpu.VMEM((SIDE * rows, width), BF16),
        ]
        + weight_scratch
        + [pltpu.SemaphoreType.DMA((SIDE * SIDE,)), pltpu.SemaphoreType.DMA((3,))],
        compiler_params=params,
        cost_estimate=pl.CostEstimate(
            flops=3 * SIDE * rows * unit, bytes_accessed=18 * 1024 * 1024, transcendentals=SIDE * rows * ff
        ),
        name="expert_forward",
    )(pos, gathered, wg, wu, wd)
    after, out = lax.optimization_barrier((pos, out))
    lines = [[z * SIDE + y for y in range(SIDE)] for z in range(SIDE)]
    outs = lax.all_to_all(
        out.reshape(SIDE, rows, width), "expert", split_axis=0, concat_axis=0, tiled=True, axis_index_groups=lines
    ).reshape(out.shape)

    steps = 2
    group, slots = everyone // steps, experts * CAP // steps
    wide = width + LANES

    def slot_spec(columns):
        return pl.BlockSpec((slots, columns), lambda i: (i, 0))

    *pieces, d_gate, d_up, gated, packed = pl.pallas_call(
        functools.partial(backward_kernel, tokens, width),
        grid=(steps,),
        out_shape=[jax.ShapeDtypeStruct((rows, wide), BF16)] * SIDE
        + [jax.ShapeDtypeStruct((experts * CAP, ff), BF16)] * 3
        + [jax.ShapeDtypeStruct((experts * CAP, 2 * width), BF16)],
        in_specs=[
            SMEM,
            pl.BlockSpec((group, 2 * width), lambda i: (i, 0)),
            pl.BlockSpec((group, LANES), lambda i: (i, table_at // LANES)),
        ]
        + [ANY] * 3,
        out_specs=[ANY] * SIDE + [slot_spec(ff)] * 3 + [slot_spec(2 * width)],
        scratch_shapes=[pltpu.VMEM((experts * CAP, wide), BF16)]
        + weight_scratch
        + [
            pltpu.SemaphoreType.DMA((3,)),
            pltpu.SemaphoreType.DMA((SIDE,)),
        ],
        compiler_params=params,
        cost_estimate=pl.CostEstimate(
            flops=5 * SIDE * rows * unit, bytes_accessed=26 * 1024 * 1024, transcendentals=SIDE * rows * ff
        ),
        name="expert_backward",
    )(after, gathered, gathered, wg, wu, wd)
    grads = [pull(pieces[d], "z", SIDE - d) for d in range(SIDE)]

    tables = gathered[:, table_at : table_at + LANES]

    def combine(at, parts, along, lane, weighted):
        wide = parts[0].shape[1]
        return pl.pallas_call(
            functools.partial(combine_kernel, tokens, along, 0, lane, weighted, len(parts) == 1),
            out_shape=[jax.ShapeDtypeStruct((SIDE * tokens // len(parts), wide), BF16)] * len(parts),
            in_specs=[SMEM, ANY] + [VMEM] * len(parts),
            out_specs=[VMEM] * len(parts),
            scratch_shapes=[pltpu.VMEM((SIDE, tokens, LANES), BF16), pltpu.SemaphoreType.DMA((SIDE,))],
            compiler_params=params,
            cost_estimate=pl.CostEstimate(
                flops=2 * SIDE * tokens * rows * wide, bytes_accessed=5 * 1024 * 1024, transcendentals=0
            ),
            name="combine_" + along,
        )(at, tables, *parts)

    partial = combine(pos, [outs], "y", experts, True)
    summands = partial[0]
    across = [[z * SIDE + y for z in range(SIDE)] for y in range(SIDE)]
    partial = lax.all_to_all(
        partial[0].reshape(SIDE, tokens, width), "expert", split_axis=0, concat_axis=0, tiled=True, axis_index_groups=across
    )
    mixed = jnp.sum(partial.astype(F32), axis=0)
    fwd_out = (arrived.astype(F32) + mixed).astype(BF16)

    grad_gate = mm(packed[:, :width], d_gate, TN).astype(BF16)
    grad_up = mm(packed[:, :width], d_up, TN).astype(BF16)
    grad_down = mm(gated, packed[:, width:], TN).astype(BF16)
    later, _ = lax.optimization_barrier((pos, (grad_gate, grad_up, grad_down, summands)))
    partial = combine(later, grads, "z", 0, False)
    summed = sum(pull(partial[d], "y", SIDE - d).astype(F32) for d in range(SIDE))

    gate_grad = jnp.sum(hit_prev * summed[:, None, width : width + experts], axis=2).astype(BF16)
    dxhat = summed[:, :width] * gain
    bwd_out = cot.astype(F32) + scale_prev * (
        dxhat - unit_prev * jnp.mean(dxhat * unit_prev, axis=-1, keepdims=True)
    )
    return (
        fwd_out[None],
        bwd_out.astype(BF16)[None],
        gate_grad[None],
        grad_gate[None, None],
        grad_up[None, None],
        grad_down[None, None],
    )


def solution(mesh):
    tokens = P("section", "expert", None)
    weight = P("section", "expert", None, None)
    return jax.shard_map(
        per_device,
        mesh=mesh,
        in_specs=(tokens, tokens, tokens, P("section", None), weight, weight, weight, tokens, tokens, tokens, tokens),
        out_specs=(tokens, tokens, tokens, weight, weight, weight),
        check_vma=False,
    )
```
